32 devices in a mesh: section: 4 (over y, x), seq: 4 (over z), dp: 2 (over core).
Axes of the slice: x: 2, y: 2, z: 4, core: 2. Of those that a mesh axis runs over, the one named last changes fastest.
Arguments:
- queries: bfloat16 [8, 512, 1280], P(('section', 'dp'), 'seq'), may hold values from -5 to 5, as said below
- key_input: bfloat16 [8, 512, 1280], P(('section', 'dp'), 'seq'), may hold values from -5 to 5
- value_input: bfloat16 [8, 512, 1280], P(('section', 'dp'), 'seq'), may hold values from -6 to 6
- residual: bfloat16 [8, 512, 1280], P(('section', 'dp'), 'seq'), may hold values from -4 to 4
- segments: int32 [8, 512], P(('section', 'dp')), may hold values from 0 to 5, never falling along the last dimension, each value on 1 to 256 neighbouring positions
- out_weight: bfloat16 [1280, 1280], replicated, may hold values from -0.15625 to 0.15625
- cotangent: bfloat16 [8, 512, 1280], P(('section', 'dp'), 'seq'), may hold values from -6 to 6
Outputs:
- mixed_out: bfloat16 [8, 512, 1280], P(('section', 'dp'), 'seq')
- weight_grad: float32 [1280, 1280], P(('section', 'dp'))
The draws below stay inside these ranges and needn't reach their ends.
Inputs may be any that keep to these rules, and one draw needn't show every extreme that they name: queries and key_input lie within -5 to 5.
All inputs are finite; a program needn't handle non-finite values.
Results may differ from the reference program's by a relative error of at most 0.015.
Values may be sent and summed in bfloat16 or wider, within the bound.
A program may use at most 64 MiB of HBM per device.

```python
import math
import jax
import jax.numpy as jnp
import numpy as np
from jax import lax

HEADS = 16
HEAD_DIM = 80
P_DEV = 128
WIDTH = 1280
MOST = 256
SEQ = 512
SAMPLES = 8
SEGS = 6
N_SEQ = 4


def draw_both(key):
    shape = (SAMPLES, SEQ, HEADS * HEAD_DIM)
    key_query, key_keys = jax.random.split(jax.random.fold_in(key, 4177), 2)
    query_draw = jnp.clip(jax.random.normal(key_query, shape, jnp.float32), -4.0, 4.0)
    keys_draw = jnp.clip(jax.random.normal(key_keys, shape, jnp.float32), -4.0, 4.0)
    return (query_draw, keys_draw)


def draw_queries(key, part):
    return draw_both(key)[0].astype(jnp.bfloat16)


def draw_key_input(key, part):
    return draw_both(key)[1].astype(jnp.bfloat16)


def strengthened(values, own_key, source, target, parts, factor):
    def block_of(axis_at):
        return (jnp.arange(values.shape[axis_at]) // (values.shape[axis_at] // parts)).reshape((-1,) + (1,) * (values.ndim - 1 - axis_at))

    first = jax.random.permutation(own_key, parts)[block_of(target)]
    second = (block_of(target) + parts // 2) % parts
    return jnp.where((block_of(source) == first) | (block_of(source) == second), factor * values, values)


def block_levels(rng, shape, pieces, smallest, high):
    gain = 1.0
    for dim, shards_of in pieces:
        steps = jax.random.uniform(jax.random.fold_in(jax.random.fold_in(rng, 6), dim), (shards_of,), jnp.float32, smallest / len(pieces), high / len(pieces))
        gain = gain * jnp.repeat(jnp.exp(steps), shape[dim] // shards_of).reshape((-1,) + (1,) * (len(shape) - 1 - dim))
    return gain


def length_profile(amount, total, limit, slope):
    loads = [(1 << 20) // math.isqrt(grade ** slope) + 1 for grade in range(2, amount + 1)]
    rest, counts = total - limit - (amount - 1), [1] * (amount - 1)
    while rest > 0:
        movable = [i for i in range(amount - 1) if counts[i] < limit]
        pool, remaining = sum([loads[i] for i in movable]), rest
        for i in movable:
            extra = min(limit - counts[i], max(1, remaining * loads[i] // pool), rest)
            counts[i] = counts[i] + extra
            rest = rest - extra
    return np.array([limit] + counts)


def uneven(key, number_of, total, most, slope):
    if number_of == 2:
        one = jax.random.randint(key, (), max(1, total - most), min(most, total - 1) + 1)
        return jnp.stack([one, total - one])
    sizes = jnp.asarray(length_profile(number_of, total, most, slope), jnp.int32)
    twos = (number_of - 1) // 2
    giver, taker = sizes[1:1 + 2 * twos:2], sizes[2:2 + 2 * twos:2]
    room = jnp.minimum(giver - 1, most - taker)
    passed = jax.random.randint(jax.random.fold_in(key, 1), (twos,), 0, 1 << 20) % (room + 1)
    sizes = sizes.at[1:1 + 2 * twos:2].set(giver - passed).at[2:2 + 2 * twos:2].set(taker + passed)
    return sizes[jax.random.permutation(jax.random.fold_in(key, 2), number_of)]


def noise(rng, shape, scale, most, cuts=(), kind=jnp.bfloat16):
    gain = block_levels(rng, shape, cuts, -0.22, 0.18) if cuts else 1.0
    array = jax.random.normal(rng, shape, jnp.float32) * scale * gain
    return jnp.minimum(jnp.maximum(array, -most), most).astype(kind)


def heavy_noise(key, shape, width, most, shards, heavy, held_as=jnp.bfloat16):
    values = width * jax.random.normal(key, shape, jnp.float32)
    if shards:
        values = values * block_levels(key, shape, shards, -0.22, 0.18)
    return jnp.clip(strengthened(values, jax.random.fold_in(key, 3), *heavy), -most, most).astype(held_as)


def setup_inputs(seed: int = 0) -> dict:
    key_of = jax.random.split(jax.random.key(seed), 8)
    queries = draw_queries(jax.random.fold_in(key_of[7], 71), 0)
    key_input = draw_key_input(jax.random.fold_in(key_of[7], 71), 0)
    value_input = noise(key_of[2], (SAMPLES, SEQ, WIDTH), 1.0, 6.0, ((0, 8), (1, 4)))
    residual = noise(key_of[3], (SAMPLES, SEQ, WIDTH), 0.5, 4.0, ((0, 8), (1, 4)))
    segments = jax.vmap(lambda own: jnp.searchsorted(jnp.cumsum(uneven(own, SEGS, SEQ, MOST, 2)), jnp.arange(SEQ), side="right"))(jax.random.split(key_of[4], SAMPLES)).reshape((SAMPLES, SEQ)).astype(jnp.int32)
    out_weight = noise(key_of[5], (WIDTH, WIDTH), WIDTH ** -0.5, 0.15625)
    cotangent = heavy_noise(key_of[6], (SAMPLES, SEQ, WIDTH), 1.0, 6.0, ((0, 8), (1, 4)), (0, 2, 8, 2.0))
    return dict(queries=queries, key_input=key_input, value_input=value_input, residual=residual, segments=segments, out_weight=out_weight, cotangent=cotangent)


def attend_sample(inputs):
    query_rows, key_rows, value_rows, image_ids = inputs
    margin = MOST
    key_padded = jnp.pad(key_rows, ((margin, margin), (0, 0)))
    value_padded = jnp.pad(value_rows, ((margin, margin), (0, 0)))
    ids_padded = jnp.pad(image_ids, (margin, margin), constant_values=-1)
    span = P_DEV + 2 * margin

    def one_block(block):
        start = (block * P_DEV).astype(jnp.int32)
        query_block = lax.dynamic_slice_in_dim(query_rows, start, P_DEV, 0).astype(jnp.float32)
        query_ids = lax.dynamic_slice_in_dim(image_ids, start, P_DEV, 0)
        key_block = lax.dynamic_slice_in_dim(key_padded, start, span, 0).astype(jnp.float32)
        value_block = lax.dynamic_slice_in_dim(value_padded, start, span, 0).astype(jnp.float32)
        key_ids = lax.dynamic_slice_in_dim(ids_padded, start, span, 0)
        query_heads = query_block.reshape(P_DEV, HEADS, HEAD_DIM)
        key_heads = key_block.reshape(span, HEADS, HEAD_DIM)
        value_heads = value_block.reshape(span, HEADS, HEAD_DIM)
        scores = jnp.einsum("qhd,khd->hqk", query_heads, key_heads) * (HEAD_DIM ** -0.5)
        usable = query_ids[:, None] == key_ids[None, :]
        scores = jnp.where(usable[None], scores, jnp.float32(-1e30))
        highest = jnp.max(scores, axis=-1, keepdims=True)
        expo = jnp.where(usable[None], jnp.exp(scores - highest), jnp.float32(0.0))
        probs = (expo / jnp.sum(expo, axis=-1, keepdims=True)).astype(jnp.bfloat16)
        attended = jnp.einsum("hqk,khd->qhd", probs.astype(jnp.float32), value_heads)
        return attended.reshape(P_DEV, HEADS * HEAD_DIM).astype(jnp.bfloat16)

    result = lax.map(one_block, jnp.arange(N_SEQ, dtype=jnp.int32))
    return result.reshape(SEQ, HEADS * HEAD_DIM)


def reference(queries, key_input, value_input, residual, segments, out_weight, cotangent):
    attended = lax.map(attend_sample, (queries, key_input, value_input, segments))
    projected = lax.dot_general(attended, out_weight, (((2,), (1,)), ((), ())), preferred_element_type=jnp.float32)
    mixed_out = (residual.astype(jnp.float32) + projected).astype(jnp.bfloat16)
    grad_scale = 1.0 / (float(SAMPLES * SEQ) ** 0.5)
    width_all = HEADS * HEAD_DIM

    def add_sample(total, inputs):
        attended_rows, grad_rows = inputs
        attended_blocks = attended_rows.reshape(N_SEQ, P_DEV, width_all).astype(jnp.float32)
        grad_blocks = grad_rows.reshape(N_SEQ, P_DEV, width_all).astype(jnp.float32)
        partial_value = (jnp.einsum("jpo,jpi->joi", grad_blocks, attended_blocks) * grad_scale).astype(jnp.bfloat16)
        return total + jnp.sum(partial_value.astype(jnp.float32), axis=0), None

    weight_grad, _ = lax.scan(add_sample, jnp.zeros((width_all, width_all), jnp.float32), (attended, cotangent))
    return mixed_out, weight_grad
```

```python
import functools
import math

import jax
import jax.numpy as jnp
from jax import lax
from jax.experimental import pallas as pl
from jax.experimental.pallas import tpu as pltpu
from jax.sharding import PartitionSpec as P

HEADS = 16
MOST = 256
LANES = 128
MESH = pl.DeviceIdType.MESH


def body(dims, q_hbm, k_hbm, v_hbm, res_hbm, seg_ref, w_hbm, cot_hbm, mix_ref, wg_ref,
         q, res, cot, w, kbuf, vbuf, cot_t, bias, att, mix, part, dp_in, pair, sec_in, acc,
         chain_out, chain_in,
         local_sem, kv_send, kv_recv, dp_send, dp_recv, sec_send, sec_recv, ch_send, ch_recv):
    N, S, D, rows, width, C, reach, R, subs = dims
    halves = width // C
    head_dim = width // HEADS
    half_heads = C // head_dim
    slots = 2 * reach + 1
    me, sec, core = lax.axis_index("seq"), lax.axis_index("section"), lax.axis_index("dp")
    towards = (1, -1)

    def can_send(direction):
        return (me < N - 1) if direction > 0 else (me > 0)

    def can_take(direction, hops):
        return (me >= hops) if direction > 0 else (me < N - hops)

    barrier = pltpu.get_barrier_semaphore()
    for direction in towards:
        @pl.when(can_send(direction))
        def _():
            pl.semaphore_signal(barrier, inc=1, device_id={"seq": me + direction}, device_id_type=MESH)
    for o in range(1, S):
        pl.semaphore_signal(barrier, inc=1, device_id={"section": lax.rem(sec + o, S)}, device_id_type=MESH)
    for o in range(1, D):
        pl.semaphore_signal(barrier, inc=1, device_id={"dp": lax.rem(core + o, D)}, device_id_type=MESH)

    own_rows = pl.ds(reach * rows, rows)
    locals_ = [
        pltpu.make_async_copy(src, dst, local_sem.at[i])
        for i, (src, dst) in enumerate((
            (cot_hbm.at[0], cot), (q_hbm.at[0], q),
            (k_hbm.at[0], kbuf.at[own_rows]), (v_hbm.at[0], vbuf.at[own_rows]),
            (res_hbm.at[0], res), (w_hbm, w)))
    ]
    for copy in locals_:
        copy.start()

    beside = (me < N - 1).astype(jnp.int32) + (me > 0).astype(jnp.int32)
    pl.semaphore_wait(barrier, beside + (S - 1) + (D - 1))

    def kv_copy(side, hop, c, kind):
        direction = towards[side]
        cols = pl.ds(c * C, C)
        buf = (kbuf, vbuf)[kind]
        if hop == 1:
            src = (k_hbm, v_hbm)[kind].at[0, :, cols]
        else:
            src = buf.at[pl.ds((reach - direction * (hop - 1)) * rows, rows), cols]
        return pltpu.make_async_remote_copy(
            src_ref=src, dst_ref=buf.at[pl.ds((reach - direction * hop) * rows, rows), cols],
            send_sem=kv_send.at[side, hop - 1, c, kind], recv_sem=kv_recv.at[side, hop - 1, c, kind],
            device_id={"seq": me + direction}, device_id_type=MESH)

    def kv_sends(side, hop):
        return can_send(towards[side]) & can_take(towards[side], hop - 1)

    for c in range(halves):
        for side in range(2):
            @pl.when(kv_sends(side, 1))
            def _():
                for kind in range(2):
                    kv_copy(side, 1, c, kind).start()

    for side in range(2):
        for hop in range(1, reach + 1):
            @pl.when(jnp.logical_not(can_take(towards[side], hop)))
            def _():
                at = pl.ds((reach - towards[side] * hop) * rows, rows)
                kbuf[at, :] = jnp.zeros((rows, width), kbuf.dtype)
                vbuf[at, :] = jnp.zeros((rows, width), vbuf.dtype)

    def ids_at(block):
        return seg_ref[:, pl.ds(pl.multiple_of(block * rows, rows), rows)].astype(jnp.float32)

    own_ids = jnp.transpose(jnp.broadcast_to(ids_at(me), (rows, rows)))
    for slot in range(slots):
        block = me + (slot - reach)
        inside = (block >= 0) & (block < N)
        ids = ids_at(jnp.clip(block, 0, N - 1))
        ids = jnp.where(inside, ids, jnp.float32(-1.0))
        bias[:, slot * rows:(slot + 1) * rows] = jnp.where(
            own_ids == jnp.broadcast_to(ids, (rows, rows)), jnp.float32(0.0), jnp.float32(-1e30))

    locals_[0].wait()
    cot_t[...] = jnp.transpose(cot[...].astype(jnp.float32)).astype(cot_t.dtype)
    att[...] = jnp.zeros_like(att)

    for hop in range(2, reach + 1):
        for c in range(halves):
            for side in range(2):
                @pl.when(can_take(towards[side], hop - 1))
                def _():
                    for kind in range(2):
                        kv_copy(side, hop - 1, c, kind).wait_recv()

                @pl.when(kv_sends(side, hop))
                def _():
                    for kind in range(2):
                        kv_copy(side, hop, c, kind).start()
    for copy in locals_[1:4]:
        copy.wait()

    fold = head_dim ** -0.5 * math.log2(math.e)

    def attention(c):
        for side in range(2):
            @pl.when(can_take(towards[side], reach))
            def _():
                for kind in range(2):
                    kv_copy(side, reach, c, kind).wait_recv()
        for head in range(c * half_heads, (c + 1) * half_heads):
            first, last = head * head_dim, (head + 1) * head_dim
            lo, hi = first // LANES * LANES, -(-last // LANES) * LANES
            lane = lax.broadcasted_iota(jnp.int32, (1, hi - lo), 1) + lo
            mine = jnp.where((lane >= first) & (lane < last), jnp.float32(1.0), jnp.float32(0.0))
            query = q[:, lo:hi] * mine.astype(jnp.bfloat16)
            scores = lax.dot_general(query, kbuf[:, lo:hi], (((1,), (1,)), ((), ())),
                                     preferred_element_type=jnp.float32)
            scores = scores * fold + bias[...]
            expo = jnp.exp2(scores - jnp.max(scores, axis=-1, keepdims=True))
            total = jnp.sum(expo, axis=-1, keepdims=True)
            out = jnp.dot(expo.astype(jnp.bfloat16), vbuf[:, lo:hi], preferred_element_type=jnp.float32)
            att[:, lo:hi] += out * (mine / total)

    def dp_copy(c, o):
        peer = lax.rem(core + o, D)
        return pltpu.make_async_remote_copy(
            src_ref=part.at[c, peer], dst_ref=dp_in.at[c, o - 1],
            send_sem=dp_send.at[c, o - 1], recv_sem=dp_recv.at[c, o - 1],
            device_id={"dp": peer}, device_id_type=MESH)

    def sec_copy(c, o):
        peer = lax.rem(sec + o, S)
        return pltpu.make_async_remote_copy(
            src_ref=pair.at[c, peer], dst_ref=sec_in.at[c, o - 1],
            send_sem=sec_send.at[c, o - 1], recv_sem=sec_recv.at[c, o - 1],
            device_id={"section": peer}, device_id_type=MESH)

    grad_scale = 1.0 / float(S * D * N * rows) ** 0.5
    tile = max(1, 640 // R)

    def partials(c):
        here = att[:, c * C:(c + 1) * C].astype(jnp.bfloat16)
        groups = S * D
        for at in range(0, groups, tile):
            count = min(tile, groups - at)
            value = jnp.dot(cot_t[at * R:(at + count) * R, :], here,
                            preferred_element_type=jnp.float32) * grad_scale
            for j in range(count):
                group = at + j
                part[c, group % D, group // D] = value[j * R:(j + 1) * R].astype(part.dtype)
        for o in range(1, D):
            dp_copy(c, o).start()

    def pair_up(c):
        for o in range(1, D):
            dp_copy(c, o).wait_recv()
        for o in [*range(1, S), 0]:
            peer = lax.rem(sec + o, S)
            value = part[c, core, peer].astype(jnp.float32)
            for p in range(1, D):
                value = value + dp_in[c, p - 1, peer].astype(jnp.float32)
            if o:
                pair[c, peer] = value.astype(pair.dtype)
                sec_copy(c, o).start()
            else:
                acc[c] = value

    edges = [(C // LANES * i // subs * LANES, C // LANES * (i + 1) // subs * LANES) for i in range(subs)]

    def chain_copy(side, c, s):
        cols = pl.ds(edges[s][0], edges[s][1] - edges[s][0])
        return pltpu.make_async_remote_copy(
            src_ref=chain_out.at[side, c, :, cols], dst_ref=chain_in.at[side, c, :, cols],
            send_sem=ch_send.at[side, c, s], recv_sem=ch_recv.at[side, c, s],
            device_id={"seq": me + towards[side]}, device_id_type=MESH)

    def chain_start(c):
        for o in range(1, S):
            sec_copy(c, o).wait_recv()
        for s, (lo, hi) in enumerate(edges):
            value = acc[c, :, lo:hi]
            for o in range(1, S):
                value = value + sec_in[c, o - 1, :, lo:hi].astype(jnp.float32)
            acc[c, :, lo:hi] = value
            for side in range(2):
                @pl.when(can_send(towards[side]) & jnp.logical_not(can_take(towards[side], 1)))
                def _():
                    chain_out[side, c, :, lo:hi] = acc[c, :, lo:hi].astype(chain_out.dtype)
                    chain_copy(side, c, s).start()
            wg_ref[:, c * C + lo:c * C + hi] = value

    def chain_rest(c):
        for s, (lo, hi) in enumerate(edges):
            for turn in range(2):
                for side in range(2):
                    near = (me * 2 < N) if side == 0 else (me * 2 >= N)
                    now = near if turn == 0 else jnp.logical_not(near)

                    @pl.when(now & can_take(towards[side], 1))
                    def _():
                        chain_copy(side, c, s).wait_recv()
                        came = chain_in[side, c, :, lo:hi].astype(jnp.float32)

                        @pl.when(can_send(towards[side]))
                        def _():
                            chain_out[side, c, :, lo:hi] = (acc[c, :, lo:hi] + came).astype(chain_out.dtype)
                            chain_copy(side, c, s).start()
                        wg_ref[:, c * C + lo:c * C + hi] += came

    def project(c):
        here = att[:, c * C:(c + 1) * C].astype(jnp.bfloat16)
        value = lax.dot_general(here, w[:, c * C:(c + 1) * C], (((1,), (1,)), ((), ())),
                                preferred_element_type=jnp.float32)
        if c == 0:
            mix[...] = res[...].astype(jnp.float32) + value
        elif c < halves - 1:
            mix[...] += value
        if c == halves - 1:
            mix_ref[0] = (mix[...] + (value if c else 0.0)).astype(mix_ref.dtype)

    for c in range(halves):
        attention(c)
        partials(c)
        if c == 0:
            for copy in locals_[4:]:
                copy.wait()
        if c < halves - 1:
            project(c)
        pair_up(c)
    project(halves - 1)
    for c in range(halves):
        chain_start(c)
        chain_rest(c)

    for c in range(halves):
        for side in range(2):
            for hop in range(1, reach + 1):
                @pl.when(kv_sends(side, hop))
                def _():
                    for kind in range(2):
                        kv_copy(side, hop, c, kind).wait_send()

            @pl.when(can_send(towards[side]))
            def _():
                for s in range(subs):
                    chain_copy(side, c, s).wait_send()
        for o in range(1, D):
            dp_copy(c, o).wait_send()
        for o in range(1, S):
            sec_copy(c, o).wait_send()


def solution(mesh):
    N, S, D = mesh.shape["seq"], mesh.shape["section"], mesh.shape["dp"]

    def per_device(queries, key_input, value_input, residual, segments, out_weight, cotangent):
        rows, width = queries.shape[1], queries.shape[2]
        head_dim = width // HEADS
        C = math.lcm(head_dim, LANES)
        halves = width // C
        reach = min(-(-(MOST - 1) // rows), N - 1)
        R = width // (S * D)
        subs = 2
        link = jnp.bfloat16 if N <= 8 else jnp.float32
        bf, f32 = jnp.bfloat16, jnp.float32
        span = (2 * reach + 1) * rows
        others, cores = max(1, S - 1), max(1, D - 1)
        dma = pltpu.SemaphoreType.DMA
        anywhere = pl.BlockSpec(memory_space=pl.ANY)
        vmem = pl.BlockSpec(memory_space=pltpu.VMEM)
        return pl.pallas_call(
            functools.partial(body, (N, S, D, rows, width, C, reach, R, subs)),
            out_shape=(jax.ShapeDtypeStruct((1, rows, width), bf), jax.ShapeDtypeStruct((R, width), f32)),
            in_specs=[anywhere] * 4 + [vmem] + [anywhere] * 2,
            out_specs=(vmem, vmem),
            scratch_shapes=[
                pltpu.VMEM((rows, width), bf), pltpu.VMEM((rows, width), bf), pltpu.VMEM((rows, width), bf),
                pltpu.VMEM((width, width), bf),
                pltpu.VMEM((span, width), bf), pltpu.VMEM((span, width), bf),
                pltpu.VMEM((width, rows), bf), pltpu.VMEM((rows, span), f32),
                pltpu.VMEM((rows, width), f32), pltpu.VMEM((rows, width), f32),
                pltpu.VMEM((halves, D, S, R, C), bf), pltpu.VMEM((halves, cores, S, R, C), bf),
                pltpu.VMEM((halves, S, R, C), bf), pltpu.VMEM((halves, others, R, C), bf),
                pltpu.VMEM((halves, R, C), f32),
                pltpu.VMEM((2, halves, R, C), link), pltpu.VMEM((2, halves, R, C), link),
                dma((6,)), dma((2, reach, halves, 2)), dma((2, reach, halves, 2)),
                dma((halves, cores)), dma((halves, cores)), dma((halves, others)), dma((halves, others)),
                dma((2, halves, subs)), dma((2, halves, subs)),
            ],
            compiler_params=pltpu.CompilerParams(
                collective_id=0, has_side_effects=True, vmem_limit_bytes=48 * 1024 * 1024),
        )(queries, key_input, value_input, residual, segments, out_weight, cotangent)

    rows_spec = P(("section", "dp"), "seq", None)
    in_specs = (rows_spec, rows_spec, rows_spec, rows_spec, P(("section", "dp"), None), P(), rows_spec)
    return jax.shard_map(per_device, mesh=mesh, in_specs=in_specs,
                         out_specs=(rows_spec, P(("section", "dp"), None)), check_vma=False)
```

```python
import functools
import math

import jax
import jax.numpy as jnp
from jax import lax
from jax.experimental import pallas as pl
from jax.experimental.pallas import tpu as pltpu
from jax.sharding import PartitionSpec as P

HEADS = 16
MOST = 256
LANES = 128
MESH = pl.DeviceIdType.MESH


def body(dims, q_hbm, k_hbm, v_hbm, res_hbm, seg_ref, w_hbm, cot_hbm, mix_ref, wg_ref,
         q, res, cot, w, kbuf, vbuf, cot_t, bias, att, mix, part, dp_in, pair, sec_in, acc,
         chain_out, chain_in,
         local_sem, kv_send, kv_recv, dp_send, dp_recv, sec_send, sec_recv, ch_send, ch_recv):
    N, S, D, rows, width, C, reach, R, step = dims
    edges = [(lo, min(C, lo + step)) for lo in range(0, C, step)]
    halves = width // C
    head_dim = width // HEADS
    half_heads = C // head_dim
    slots = 2 * reach + 1
    me, sec, core = lax.axis_index("seq"), lax.axis_index("section"), lax.axis_index("dp")
    towards = (1, -1)

    def can_send(direction):
        return (me < N - 1) if direction > 0 else (me > 0)

    def can_take(direction, hops):
        return (me >= hops) if direction > 0 else (me < N - hops)

    barrier = pltpu.get_barrier_semaphore()
    for direction in towards:
        @pl.when(can_send(direction))
        def _():
            pl.semaphore_signal(barrier, inc=1, device_id={"seq": me + direction}, device_id_type=MESH)
    for o in range(1, S):
        pl.semaphore_signal(barrier, inc=1, device_id={"section": lax.rem(sec + o, S)}, device_id_type=MESH)
    for o in range(1, D):
        pl.semaphore_signal(barrier, inc=1, device_id={"dp": lax.rem(core + o, D)}, device_id_type=MESH)

    own_rows = pl.ds(reach * rows, rows)
    locals_ = [
        pltpu.make_async_copy(src, dst, local_sem.at[i])
        for i, (src, dst) in enumerate((
            (cot_hbm.at[0], cot), (q_hbm.at[0], q),
            (k_hbm.at[0], kbuf.at[own_rows]), (v_hbm.at[0], vbuf.at[own_rows]),
            (res_hbm.at[0], res), (w_hbm, w)))
    ]
    for copy in locals_:
        copy.start()

    beside = (me < N - 1).astype(jnp.int32) + (me > 0).astype(jnp.int32)
    pl.semaphore_wait(barrier, beside + (S - 1) + (D - 1))

    def kv_copy(side, hop, c, kind):
        direction = towards[side]
        cols = pl.ds(c * C, C)
        buf = (kbuf, vbuf)[kind]
        if hop == 1:
            src = (k_hbm, v_hbm)[kind].at[0, :, cols]
        else:
            src = buf.at[pl.ds((reach - direction * (hop - 1)) * rows, rows), cols]
        return pltpu.make_async_remote_copy(
            src_ref=src, dst_ref=buf.at[pl.ds((reach - direction * hop) * rows, rows), cols],
            send_sem=kv_send.at[side, hop - 1, c, kind], recv_sem=kv_recv.at[side, hop - 1, c, kind],
            device_id={"seq": me + direction}, device_id_type=MESH)

    def kv_sends(side, hop):
        return can_send(towards[side]) & can_take(towards[side], hop - 1)

    for c in range(halves):
        for side in range(2):
            @pl.when(kv_sends(side, 1))
            def _():
                for kind in range(2):
                    kv_copy(side, 1, c, kind).start()

    for side in range(2):
        for hop in range(1, reach + 1):
            @pl.when(jnp.logical_not(can_take(towards[side], hop)))
            def _():
                at = pl.ds((reach - towards[side] * hop) * rows, rows)
                kbuf[at, :] = jnp.zeros((rows, width), kbuf.dtype)
                vbuf[at, :] = jnp.zeros((rows, width), vbuf.dtype)

    def ids_at(block):
        return seg_ref[:, pl.ds(pl.multiple_of(block * rows, rows), rows)].astype(jnp.float32)

    own_ids = jnp.transpose(jnp.broadcast_to(ids_at(me), (rows, rows)))
    for slot in range(slots):
        block = me + (slot - reach)
        inside = (block >= 0) & (block < N)
        ids = ids_at(jnp.clip(block, 0, N - 1))
        ids = jnp.where(inside, ids, jnp.float32(-1.0))
        bias[:, slot * rows:(slot + 1) * rows] = jnp.where(
            own_ids == jnp.broadcast_to(ids, (rows, rows)), jnp.float32(0.0), jnp.float32(-1e30))

    locals_[0].wait()
    cot_t[...] = jnp.transpose(cot[...].astype(jnp.float32)).astype(cot_t.dtype)
    att[...] = jnp.zeros_like(att)

    for hop in range(2, reach + 1):
        for c in range(halves):
            for side in range(2):
                @pl.when(can_take(towards[side], hop - 1))
                def _():
                    for kind in range(2):
                        kv_copy(side, hop - 1, c, kind).wait_recv()

                @pl.when(kv_sends(side, hop))
                def _():
                    for kind in range(2):
                        kv_copy(side, hop, c, kind).start()
    for copy in locals_[1:4]:
        copy.wait()

    fold = head_dim ** -0.5 * math.log2(math.e)

    def attention(c):
        for side in range(2):
            @pl.when(can_take(towards[side], reach))
            def _():
                for kind in range(2):
                    kv_copy(side, reach, c, kind).wait_recv()
        for head in range(c * half_heads, (c + 1) * half_heads):
            first, last = head * head_dim, (head + 1) * head_dim
            lo, hi = first // LANES * LANES, -(-last // LANES) * LANES
            lane = lax.broadcasted_iota(jnp.int32, (1, hi - lo), 1) + lo
            mine = jnp.where((lane >= first) & (lane < last), jnp.float32(1.0), jnp.float32(0.0))
            query = q[:, lo:hi] * mine.astype(jnp.bfloat16)
            scores = lax.dot_general(query, kbuf[:, lo:hi], (((1,), (1,)), ((), ())),
                                     preferred_element_type=jnp.float32)
            scores = scores * fold + bias[...]
            expo = jnp.exp2(scores - jnp.max(scores, axis=-1, keepdims=True))
            total = jnp.sum(expo, axis=-1, keepdims=True)
            out = jnp.dot(expo.astype(jnp.bfloat16), vbuf[:, lo:hi], preferred_element_type=jnp.float32)
            att[:, lo:hi] += out * (mine / total)

    def columns(s):
        return pl.ds(edges[s][0], edges[s][1] - edges[s][0])

    def dp_copy(c, s, o):
        peer = lax.rem(core + o, D)
        return pltpu.make_async_remote_copy(
            src_ref=part.at[c, peer, :, :, columns(s)], dst_ref=dp_in.at[c, o - 1, :, :, columns(s)],
            send_sem=dp_send.at[c, s, o - 1], recv_sem=dp_recv.at[c, s, o - 1],
            device_id={"dp": peer}, device_id_type=MESH)

    def sec_copy(c, s, o):
        peer = lax.rem(sec + o, S)
        return pltpu.make_async_remote_copy(
            src_ref=pair.at[c, peer, :, columns(s)], dst_ref=sec_in.at[c, o - 1, :, columns(s)],
            send_sem=sec_send.at[c, s, o - 1], recv_sem=sec_recv.at[c, s, o - 1],
            device_id={"section": peer}, device_id_type=MESH)

    def chain_copy(side, c, s):
        return pltpu.make_async_remote_copy(
            src_ref=chain_out.at[side, c, :, columns(s)], dst_ref=chain_in.at[side, c, :, columns(s)],
            send_sem=ch_send.at[side, c, s], recv_sem=ch_recv.at[side, c, s],
            device_id={"seq": me + towards[side]}, device_id_type=MESH)

    grad_scale = 1.0 / float(S * D * N * rows) ** 0.5
    tile = max(1, 640 // R)

    def partials(c, s):
        lo, hi = edges[s]
        here = att[:, c * C + lo:c * C + hi].astype(jnp.bfloat16)
        groups = S * D
        for at in range(0, groups, tile):
            count = min(tile, groups - at)
            value = jnp.dot(cot_t[at * R:(at + count) * R, :], here,
                            preferred_element_type=jnp.float32) * grad_scale
            for j in range(count):
                group = at + j
                part[c, group % D, group // D, :, lo:hi] = value[j * R:(j + 1) * R].astype(part.dtype)
        for o in range(1, D):
            dp_copy(c, s, o).start()

    def pair_up(c, s):
        lo, hi = edges[s]
        for o in range(1, D):
            dp_copy(c, s, o).wait_recv()
        for o in [*range(1, S), 0]:
            peer = lax.rem(sec + o, S)
            value = part[c, core, peer, :, lo:hi].astype(jnp.float32)
            for p in range(1, D):
                value = value + dp_in[c, p - 1, peer, :, lo:hi].astype(jnp.float32)
            if o:
                pair[c, peer, :, lo:hi] = value.astype(pair.dtype)
                sec_copy(c, s, o).start()
            else:
                acc[c, :, lo:hi] = value

    def chain_start(c, s):
        lo, hi = edges[s]
        for o in range(1, S):
            sec_copy(c, s, o).wait_recv()
        value = acc[c, :, lo:hi]
        for o in range(1, S):
            value = value + sec_in[c, o - 1, :, lo:hi].astype(jnp.float32)
        acc[c, :, lo:hi] = value
        for side in range(2):
            @pl.when(can_send(towards[side]) & jnp.logical_not(can_take(towards[side], 1)))
            def _():
                chain_out[side, c, :, lo:hi] = acc[c, :, lo:hi].astype(chain_out.dtype)
                chain_copy(side, c, s).start()
        wg_ref[:, c * C + lo:c * C + hi] = value

    def chain_step(c, s, turn):
        lo, hi = edges[s]
        for side in range(2):
            near = (me * 2 < N) if side == 0 else (me * 2 >= N)
            now = near if turn == 0 else jnp.logical_not(near)

            @pl.when(now & can_take(towards[side], 1))
            def _():
                chain_copy(side, c, s).wait_recv()
                came = chain_in[side, c, :, lo:hi].astype(jnp.float32)

                @pl.when(can_send(towards[side]))
                def _():
                    chain_out[side, c, :, lo:hi] = (acc[c, :, lo:hi] + came).astype(chain_out.dtype)
                    chain_copy(side, c, s).start()
                wg_ref[:, c * C + lo:c * C + hi] += came

    def project(c):
        here = att[:, c * C:(c + 1) * C].astype(jnp.bfloat16)
        value = lax.dot_general(here, w[:, c * C:(c + 1) * C], (((1,), (1,)), ((), ())),
                                preferred_element_type=jnp.float32)
        if c == 0:
            mix[...] = res[...].astype(jnp.float32) + value
        elif c < halves - 1:
            mix[...] += value
        if c == halves - 1:
            mix_ref[0] = (mix[...] + (value if c else 0.0)).astype(mix_ref.dtype)

    pieces = [(c, s) for c in range(halves) for s in range(len(edges))]
    for c in range(halves):
        attention(c)
        for s in range(len(edges)):
            partials(c, s)
        if c == 0:
            for copy in locals_[4:]:
                copy.wait()
        if c < halves - 1:
            project(c)
        for s in range(len(edges)):
            pair_up(c, s)
    project(halves - 1)
    for at in range(len(pieces) + 1):
        if at < len(pieces):
            chain_start(*pieces[at])
            chain_step(*pieces[at], 0)
        if at > 0:
            chain_step(*pieces[at - 1], 1)

    for c in range(halves):
        for side in range(2):
            for hop in range(1, reach + 1):
                @pl.when(kv_sends(side, hop))
                def _():
                    for kind in range(2):
                        kv_copy(side, hop, c, kind).wait_send()

            @pl.when(can_send(towards[side]))
            def _():
                for s in range(len(edges)):
                    chain_copy(side, c, s).wait_send()
        for s in range(len(edges)):
            for o in range(1, D):
                dp_copy(c, s, o).wait_send()
            for o in range(1, S):
                sec_copy(c, s, o).wait_send()


def solution(mesh):
    N, S, D = mesh.shape["seq"], mesh.shape["section"], mesh.shape["dp"]

    def per_device(queries, key_input, value_input, residual, segments, out_weight, cotangent):
        rows, width = queries.shape[1], queries.shape[2]
        head_dim = width // HEADS
        C = math.lcm(head_dim, LANES)
        halves = width // C
        reach = min(-(-(MOST - 1) // rows), N - 1)
        R = width // (S * D)
        step = C
        subs = -(-C // step)
        link = jnp.bfloat16 if N <= 8 else jnp.float32
        bf, f32 = jnp.bfloat16, jnp.float32
        span = (2 * reach + 1) * rows
        others, cores = max(1, S - 1), max(1, D - 1)
        dma = pltpu.SemaphoreType.DMA
        anywhere = pl.BlockSpec(memory_space=pl.ANY)
        vmem = pl.BlockSpec(memory_space=pltpu.VMEM)
        return pl.pallas_call(
            functools.partial(body, (N, S, D, rows, width, C, reach, R, step)),
            out_shape=(jax.ShapeDtypeStruct((1, rows, width), bf), jax.ShapeDtypeStruct((R, width), f32)),
            in_specs=[anywhere] * 4 + [vmem] + [anywhere] * 2,
            out_specs=(vmem, vmem),
            scratch_shapes=[
                pltpu.VMEM((rows, width), bf), pltpu.VMEM((rows, width), bf), pltpu.VMEM((rows, width), bf),
                pltpu.VMEM((width, width), bf),
                pltpu.VMEM((span, width), bf), pltpu.VMEM((span, width), bf),
                pltpu.VMEM((width, rows), bf), pltpu.VMEM((rows, span), f32),
                pltpu.VMEM((rows, width), f32), pltpu.VMEM((rows, width), f32),
                pltpu.VMEM((halves, D, S, R, C), bf), pltpu.VMEM((halves, cores, S, R, C), bf),
                pltpu.VMEM((halves, S, R, C), bf), pltpu.VMEM((halves, others, R, C), bf),
                pltpu.VMEM((halves, R, C), f32),
                pltpu.VMEM((2, halves, R, C), link), pltpu.VMEM((2, halves, R, C), link),
                dma((6,)), dma((2, reach, halves, 2)), dma((2, reach, halves, 2)),
                dma((halves, subs, cores)), dma((halves, subs, cores)),
                dma((halves, subs, others)), dma((halves, subs, others)),
                dma((2, halves, subs)), dma((2, halves, subs)),
            ],
            compiler_params=pltpu.CompilerParams(
                collective_id=0, has_side_effects=True, vmem_limit_bytes=62 * 1024 * 1024),
        )(queries, key_input, value_input, residual, segments, out_weight, cotangent)

    rows_spec = P(("section", "dp"), "seq", None)
    in_specs = (rows_spec, rows_spec, rows_spec, rows_spec, P(("section", "dp"), None), P(), rows_spec)
    return jax.shard_map(per_device, mesh=mesh, in_specs=in_specs,
                         out_specs=(rows_spec, P(("section", "dp"), None)), check_vma=False)
```

```python
import functools
import math

import jax
import jax.numpy as jnp
from jax import lax
from jax.experimental import pallas as pl
from jax.experimental.pallas import tpu as pltpu
from jax.sharding import PartitionSpec as P

HEADS = 16
MOST = 256
LANES = 128
MESH = pl.DeviceIdType.MESH


def body(dims, q_hbm, k_hbm, v_hbm, res_hbm, seg_ref, w_hbm, cot_hbm, mix_ref, wg_ref,
         q, res, cot, w, kbuf, vbuf, cot_t, bias, att, mix, part, dp_in, pair, sec_in, acc,
         chain_out, chain_in,
         local_sem, kv_send, kv_recv, dp_send, dp_recv, sec_send, sec_recv, ch_send, ch_recv):
    N, S, D, rows, width, C, reach, R, step = dims
    edges = [(lo, min(C, lo + step)) for lo in range(0, C, step)]
    halves = width // C
    head_dim = width // HEADS
    half_heads = C // head_dim
    slots = 2 * reach + 1
    me, sec, core = lax.axis_index("seq"), lax.axis_index("section"), lax.axis_index("dp")
    towards = (1, -1)

    def can_send(direction):
        return (me < N - 1) if direction > 0 else (me > 0)

    def can_take(direction, hops):
        return (me >= hops) if direction > 0 else (me < N - hops)

    barrier = pltpu.get_barrier_semaphore()
    for direction in towards:
        @pl.when(can_send(direction))
        def _():
            pl.semaphore_signal(barrier, inc=1, device_id={"seq": me + direction}, device_id_type=MESH)
    for o in range(1, S):
        pl.semaphore_signal(barrier, inc=1, device_id={"section": lax.rem(sec + o, S)}, device_id_type=MESH)
    for o in range(1, D):
        pl.semaphore_signal(barrier, inc=1, device_id={"dp": lax.rem(core + o, D)}, device_id_type=MESH)

    own_rows = pl.ds(reach * rows, rows)
    locals_ = [
        pltpu.make_async_copy(src, dst, local_sem.at[i])
        for i, (src, dst) in enumerate((
            (cot_hbm.at[0], cot), (q_hbm.at[0], q),
            (k_hbm.at[0], kbuf.at[own_rows]), (v_hbm.at[0], vbuf.at[own_rows]),
            (res_hbm.at[0], res), (w_hbm, w)))
    ]
    for copy in locals_:
        copy.start()

    beside = (me < N - 1).astype(jnp.int32) + (me > 0).astype(jnp.int32)
    pl.semaphore_wait(barrier, beside + (S - 1) + (D - 1))

    def kv_copy(side, hop, c, kind):
        direction = towards[side]
        cols = pl.ds(c * C, C)
        buf = (kbuf, vbuf)[kind]
        if hop == 1:
            src = (k_hbm, v_hbm)[kind].at[0, :, cols]
        else:
            src = buf.at[pl.ds((reach - direction * (hop - 1)) * rows, rows), cols]
        return pltpu.make_async_remote_copy(
            src_ref=src, dst_ref=buf.at[pl.ds((reach - direction * hop) * rows, rows), cols],
            send_sem=kv_send.at[side, hop - 1, c, kind], recv_sem=kv_recv.at[side, hop - 1, c, kind],
            device_id={"seq": me + direction}, device_id_type=MESH)

    def kv_sends(side, hop):
        return can_send(towards[side]) & can_take(towards[side], hop - 1)

    for c in range(halves):
        for side in range(2):
            @pl.when(kv_sends(side, 1))
            def _():
                for kind in range(2):
                    kv_copy(side, 1, c, kind).start()

    for side in range(2):
        for hop in range(1, reach + 1):
            @pl.when(jnp.logical_not(can_take(towards[side], hop)))
            def _():
                at = pl.ds((reach - towards[side] * hop) * rows, rows)
                kbuf[at, :] = jnp.zeros((rows, width), kbuf.dtype)
                vbuf[at, :] = jnp.zeros((rows, width), vbuf.dtype)

    def ids_at(block):
        return seg_ref[:, pl.ds(pl.multiple_of(block * rows, rows), rows)].astype(jnp.float32)

    own_ids = jnp.transpose(jnp.broadcast_to(ids_at(me), (rows, rows)))
    for slot in range(slots):
        block = me + (slot - reach)
        inside = (block >= 0) & (block < N)
        ids = ids_at(jnp.clip(block, 0, N - 1))
        ids = jnp.where(inside, ids, jnp.float32(-1.0))
        bias[:, slot * rows:(slot + 1) * rows] = jnp.where(
            own_ids == jnp.broadcast_to(ids, (rows, rows)), jnp.float32(0.0), jnp.float32(-1e30))

    locals_[0].wait()
    cot_t[...] = jnp.transpose(cot[...].astype(jnp.float32)).astype(cot_t.dtype)
    att[...] = jnp.zeros_like(att)

    for hop in range(2, reach + 1):
        for c in range(halves):
            for side in range(2):
                @pl.when(can_take(towards[side], hop - 1))
                def _():
                    for kind in range(2):
                        kv_copy(side, hop - 1, c, kind).wait_recv()

                @pl.when(kv_sends(side, hop))
                def _():
                    for kind in range(2):
                        kv_copy(side, hop, c, kind).start()
    for copy in locals_[1:4]:
        copy.wait()

    fold = head_dim ** -0.5 * math.log2(math.e)

    def attention(c):
        for side in range(2):
            @pl.when(can_take(towards[side], reach))
            def _():
                for kind in range(2):
                    kv_copy(side, reach, c, kind).wait_recv()
        for head in range(c * half_heads, (c + 1) * half_heads):
            first, last = head * head_dim, (head + 1) * head_dim
            lo, hi = first // LANES * LANES, -(-last // LANES) * LANES
            lane = lax.broadcasted_iota(jnp.int32, (1, hi - lo), 1) + lo
            mine = jnp.where((lane >= first) & (lane < last), jnp.float32(1.0), jnp.float32(0.0))
            query = q[:, lo:hi] * mine.astype(jnp.bfloat16)
            scores = lax.dot_general(query, kbuf[:, lo:hi], (((1,), (1,)), ((), ())),
                                     preferred_element_type=jnp.float32)
            scores = scores * fold + bias[...]
            expo = jnp.exp2(scores - jnp.max(scores, axis=-1, keepdims=True))
            total = jnp.sum(expo, axis=-1, keepdims=True)
            out = jnp.dot(expo.astype(jnp.bfloat16), vbuf[:, lo:hi], preferred_element_type=jnp.float32)
            att[:, lo:hi] += out * (mine / total)

    def columns(s):
        return pl.ds(edges[s][0], edges[s][1] - edges[s][0])

    def dp_copy(c, s, o):
        peer = lax.rem(core + o, D)
        return pltpu.make_async_remote_copy(
            src_ref=part.at[c, peer, :, :, columns(s)], dst_ref=dp_in.at[c, o - 1, :, :, columns(s)],
            send_sem=dp_send.at[c, s, o - 1], recv_sem=dp_recv.at[c, s, o - 1],
            device_id={"dp": peer}, device_id_type=MESH)

    def sec_copy(c, s, o):
        peer = lax.rem(sec + o, S)
        return pltpu.make_async_remote_copy(
            src_ref=pair.at[c, peer, :, columns(s)], dst_ref=sec_in.at[c, o - 1, :, columns(s)],
            send_sem=sec_send.at[c, s, o - 1], recv_sem=sec_recv.at[c, s, o - 1],
            device_id={"section": peer}, device_id_type=MESH)

    def chain_copy(side, c, s):
        return pltpu.make_async_remote_copy(
            src_ref=chain_out.at[side, c, :, columns(s)], dst_ref=chain_in.at[side, c, :, columns(s)],
            send_sem=ch_send.at[side, c, s], recv_sem=ch_recv.at[side, c, s],
            device_id={"seq": me + towards[side]}, device_id_type=MESH)

    grad_scale = 1.0 / float(S * D * N * rows) ** 0.5
    tile = max(1, 640 // R)

    def partials(c, s):
        lo, hi = edges[s]
        here = att[:, c * C + lo:c * C + hi].astype(jnp.bfloat16)
        groups = S * D
        for at in range(0, groups, tile):
            count = min(tile, groups - at)
            value = jnp.dot(cot_t[at * R:(at + count) * R, :], here,
                            preferred_element_type=jnp.float32) * grad_scale
            for j in range(count):
                group = at + j
                part[c, group % D, group // D, :, lo:hi] = value[j * R:(j + 1) * R].astype(part.dtype)
        for o in range(1, D):
            dp_copy(c, s, o).start()

    def pair_up(c, s):
        lo, hi = edges[s]
        for o in range(1, D):
            dp_copy(c, s, o).wait_recv()
        for o in [*range(1, S), 0]:
            peer = lax.rem(sec + o, S)
            value = part[c, core, peer, :, lo:hi].astype(jnp.float32)
            for p in range(1, D):
                value = value + dp_in[c, p - 1, peer, :, lo:hi].astype(jnp.float32)
            if o:
                pair[c, peer, :, lo:hi] = value.astype(pair.dtype)
                sec_copy(c, s, o).start()
            else:
                acc[c, :, lo:hi] = value

    def chain_start(c, s):
        lo, hi = edges[s]
        for o in range(1, S):
            sec_copy(c, s, o).wait_recv()
        value = acc[c, :, lo:hi]
        for o in range(1, S):
            value = value + sec_in[c, o - 1, :, lo:hi].astype(jnp.float32)
        acc[c, :, lo:hi] = value
        for side in range(2):
            @pl.when(can_send(towards[side]) & jnp.logical_not(can_take(towards[side], 1)))
            def _():
                chain_out[side, c, :, lo:hi] = acc[c, :, lo:hi].astype(chain_out.dtype)
                chain_copy(side, c, s).start()
        wg_ref[:, c * C + lo:c * C + hi] = value

    def chain_step(c, s, turn):
        lo, hi = edges[s]
        for side in range(2):
            near = (me * 2 < N) if side == 0 else (me * 2 >= N)
            now = near if turn == 0 else jnp.logical_not(near)

            @pl.when(now & can_take(towards[side], 1))
            def _():
                chain_copy(side, c, s).wait_recv()
                came = chain_in[side, c, :, lo:hi].astype(jnp.float32)

                @pl.when(can_send(towards[side]))
                def _():
                    chain_out[side, c, :, lo:hi] = (acc[c, :, lo:hi] + came).astype(chain_out.dtype)
                    chain_copy(side, c, s).start()
                wg_ref[:, c * C + lo:c * C + hi] += came

    def project(c):
        here = att[:, c * C:(c + 1) * C].astype(jnp.bfloat16)
        value = lax.dot_general(here, w[:, c * C:(c + 1) * C], (((1,), (1,)), ((), ())),
                                preferred_element_type=jnp.float32)
        if c == 0:
            mix[...] = res[...].astype(jnp.float32) + value
        elif c < halves - 1:
            mix[...] += value
        if c == halves - 1:
            mix_ref[0] = (mix[...] + (value if c else 0.0)).astype(mix_ref.dtype)

    pieces = [(c, s) for c in range(halves) for s in range(len(edges))]
    for c in range(halves):
        attention(c)
        for s in range(len(edges)):
            partials(c, s)
        if c == 0:
            for copy in locals_[4:]:
                copy.wait()
        if c < halves - 1:
            project(c)
        for s in range(len(edges)):
            pair_up(c, s)
    project(halves - 1)
    for at in range(len(pieces) + 1):
        if at < len(pieces):
            chain_start(*pieces[at])
        if at > 0:
            chain_step(*pieces[at - 1], 1)
        if at < len(pieces):
            chain_step(*pieces[at], 0)

    for c in range(halves):
        for side in range(2):
            for hop in range(1, reach + 1):
                @pl.when(kv_sends(side, hop))
                def _():
                    for kind in range(2):
                        kv_copy(side, hop, c, kind).wait_send()

            @pl.when(can_send(towards[side]))
            def _():
                for s in range(len(edges)):
                    chain_copy(side, c, s).wait_send()
        for s in range(len(edges)):
            for o in range(1, D):
                dp_copy(c, s, o).wait_send()
            for o in range(1, S):
                sec_copy(c, s, o).wait_send()


def solution(mesh):
    N, S, D = mesh.shape["seq"], mesh.shape["section"], mesh.shape["dp"]

    def per_device(queries, key_input, value_input, residual, segments, out_weight, cotangent):
        rows, width = queries.shape[1], queries.shape[2]
        head_dim = width // HEADS
        C = math.lcm(head_dim, LANES)
        halves = width // C
        reach = min(-(-(MOST - 1) // rows), N - 1)
        R = width // (S * D)
        step = C
        subs = -(-C // step)
        link = jnp.bfloat16 if N <= 8 else jnp.float32
        bf, f32 = jnp.bfloat16, jnp.float32
        span = (2 * reach + 1) * rows
        others, cores = max(1, S - 1), max(1, D - 1)
        dma = pltpu.SemaphoreType.DMA
        anywhere = pl.BlockSpec(memory_space=pl.ANY)
        vmem = pl.BlockSpec(memory_space=pltpu.VMEM)
        return pl.pallas_call(
            functools.partial(body, (N, S, D, rows, width, C, reach, R, step)),
            out_shape=(jax.ShapeDtypeStruct((1, rows, width), bf), jax.ShapeDtypeStruct((R, width), f32)),
            in_specs=[anywhere] * 4 + [vmem] + [anywhere] * 2,
            out_specs=(vmem, vmem),
            scratch_shapes=[
                pltpu.VMEM((rows, width), bf), pltpu.VMEM((rows, width), bf), pltpu.VMEM((rows, width), bf),
                pltpu.VMEM((width, width), bf),
                pltpu.VMEM((span, width), bf), pltpu.VMEM((span, width), bf),
                pltpu.VMEM((width, rows), bf), pltpu.VMEM((rows, span), f32),
                pltpu.VMEM((rows, width), f32), pltpu.VMEM((rows, width), f32),
                pltpu.VMEM((halves, D, S, R, C), bf), pltpu.VMEM((halves, cores, S, R, C), bf),
                pltpu.VMEM((halves, S, R, C), bf), pltpu.VMEM((halves, others, R, C), bf),
                pltpu.VMEM((halves, R, C), f32),
                pltpu.VMEM((2, halves, R, C), link), pltpu.VMEM((2, halves, R, C), link),
                dma((6,)), dma((2, reach, halves, 2)), dma((2, reach, halves, 2)),
                dma((halves, subs, cores)), dma((halves, subs, cores)),
                dma((halves, subs, others)), dma((halves, subs, others)),
                dma((2, halves, subs)), dma((2, halves, subs)),
            ],
            compiler_params=pltpu.CompilerParams(
                collective_id=0, has_side_effects=True, vmem_limit_bytes=62 * 1024 * 1024),
        )(queries, key_input, value_input, residual, segments, out_weight, cotangent)

    rows_spec = P(("section", "dp"), "seq", None)
    in_specs = (rows_spec, rows_spec, rows_spec, rows_spec, P(("section", "dp"), None), P(), rows_spec)
    return jax.shard_map(per_device, mesh=mesh, in_specs=in_specs,
                         out_specs=(rows_spec, P(("section", "dp"), None)), check_vma=False)
```
